32 devices in a mesh: tok: 16 (over z, y, x), feat: 2 (over core).
Axes of the slice: x: 2, y: 2, z: 4, core: 2. Of those that a mesh axis runs over, the one named last changes fastest.
Arguments:
- hidden_states: bfloat16 [27648, 8192], P('tok', 'feat'), may hold values from -60 to 60
- current_block: float32 [8192, 64], P('feat'), may hold values from -0.0625 to 0.0625
- directions: float32 [8192, 64], P('feat'), may hold values from -0.0625 to 0.0625
Outputs:
- block_image: float32 [8192, 192], P('feat')
- gram_image: float32 [192, 192], replicated
- gram_search: float32 [192, 192], replicated
The draws below stay inside these ranges and needn't reach their ends.
All inputs are finite; a program needn't handle non-finite values.
Results may differ from the reference program's by a relative error of at most 0.005.
Values may be sent and summed in bfloat16 or wider, within the bound.
A program may use at most 64 MiB of HBM per device.

```python
import math
import jax
import jax.numpy as jnp
from jax import lax

D = 8192
KX = 64
LAG = 256
TOKENS = 27648


def draw_hidden_states(key, part):
    key_base = jax.random.fold_in(key, 11)
    key_rows = jax.random.fold_in(key, 12)
    key_cols = jax.random.fold_in(key, 13)
    position = jnp.arange(TOKENS, dtype=jnp.float32) / TOKENS
    feature = jnp.arange(D, dtype=jnp.float32) / D
    row_scale = jnp.exp(jax.random.uniform(key_rows, (TOKENS, 1), jnp.float32, -1.15, 1.15)) * jnp.sqrt(1.0 + 2.0 * position)[:, None]
    col_scale = jnp.exp(jax.random.uniform(key_cols, (1, D), jnp.float32, -0.69, 0.69)) * jnp.sqrt(1.0 + 2.0 * feature)[None, :]
    base = jnp.clip(jax.random.normal(key_base, (TOKENS, D), jnp.float32), -6.0, 6.0)
    values = jnp.clip(0.5 * base * row_scale * col_scale, -60.0, 60.0)
    return values.astype(jnp.bfloat16)


def block_scale(stream_key, extent, pieces, low, largest):
    factor_of, own = 1.0, jax.random.fold_in(stream_key, 6)
    for axis_at, blocks in pieces:
        steps = jnp.exp(jax.random.uniform(jax.random.fold_in(own, axis_at), (blocks,), jnp.float32, low / len(pieces), largest / len(pieces)))
        factor_of = factor_of * jnp.repeat(steps, extent[axis_at] // blocks).reshape([-1 if axis == axis_at else 1 for axis in range(len(extent))])
    return factor_of


def scatter_about(rng, dims, width, most, cuts=(), held_as=jnp.bfloat16):
    drawn = jax.random.normal(rng, dims, jnp.float32) * width
    if len(cuts) > 0:
        drawn = block_scale(rng, dims, cuts, -0.22, 0.18) * drawn
    return jnp.clip(drawn, min=-most, max=most).astype(held_as)


def setup_inputs(seed: int = 0) -> dict:
    seeds = jax.random.split(jax.random.key(seed), 4)
    return {
        "hidden_states": draw_hidden_states(jax.random.fold_in(seeds[3], 71), 0),
        "current_block": scatter_about(seeds[1], (D, KX), D ** -0.5, 0.0625, ((0, 2),), jnp.float32),
        "directions": scatter_about(seeds[2], (D, KX), D ** -0.5, 0.0625, ((0, 2),), jnp.float32),
    }


def lagged_apply(hidden_states, column_block):
    vectors = column_block.astype(jnp.bfloat16)
    projected = jnp.dot(hidden_states, vectors, preferred_element_type=jnp.float32)
    padding = jnp.zeros((LAG, projected.shape[1]), jnp.float32)
    ahead = jnp.concatenate([projected[LAG:], padding], axis=0)
    behind = jnp.concatenate([padding, projected[:-LAG]], axis=0)
    lagged = (ahead + behind).astype(jnp.bfloat16)
    backward = lax.dot_general(hidden_states, lagged, (((0,), (0,)), ((), ())), preferred_element_type=jnp.float32)
    return backward * (0.5 / math.sqrt(TOKENS - LAG))

def reference(hidden_states, current_block, directions):
    highest = lax.Precision.HIGHEST
    image_x = lagged_apply(hidden_states, current_block)
    rayleigh = jnp.dot(current_block.T, image_x, precision=highest)
    residual = image_x - jnp.dot(current_block, rayleigh, precision=highest)
    lengths = lax.optimization_barrier(jnp.sum(residual * residual, axis=0, keepdims=True))
    unit_residual = residual * lax.rsqrt(lengths + 1e-06)
    image_r = lagged_apply(hidden_states, unit_residual)
    image_p = lagged_apply(hidden_states, directions)
    block_image = jnp.concatenate([image_x, image_r, image_p], axis=1)
    search = jnp.concatenate([current_block, unit_residual, directions], axis=1)
    gram_image = jnp.dot(search.T, block_image, precision=highest)
    gram_search = jnp.dot(search.T, search, precision=highest)
    return (block_image, gram_image, gram_search)
```

```python
import functools
import math

import jax
import jax.numpy as jnp
from jax import lax
from jax.experimental import pallas as pl
from jax.experimental.pallas import tpu as pltpu
from jax.sharding import PartitionSpec as P

LAG = 256


def extended(value, sides, width):
    for axis, dim in sides:
        count, length = (lax.axis_size(axis), value.shape[dim])
        up = [(i, (i + 1) % count) for i in range(count - 1)]
        down = [(j, i) for i, j in up]
        last = lax.slice_in_dim(value, length - width, length, axis=dim)
        initial = lax.slice_in_dim(value, 0, width, axis=dim)
        before = lax.ppermute(last, axis, up)
        after = lax.ppermute(initial, axis, down)
        value = jnp.concatenate([before, value, after], axis=dim)
    return value


def local(hidden_states, current_block, directions):
    highest = lax.Precision.HIGHEST
    tok_count = hidden_states.shape[0]
    block_cols = current_block.shape[1]
    tokens_all = tok_count * lax.axis_size("tok")
    factor = 0.5 / math.sqrt(tokens_all - LAG)

    def project(vectors):
        partial_value = jnp.dot(hidden_states, vectors, preferred_element_type=jnp.float32)
        projected = lax.psum(partial_value, "feat")
        padded = extended(projected, (("tok", 0),), LAG)
        lagged = (padded[2 * LAG : 2 * LAG + tok_count] + padded[:tok_count]).astype(jnp.bfloat16)
        backward = lax.dot_general(
            hidden_states, lagged, (((0,), (0,)), ((), ())), preferred_element_type=jnp.float32
        )
        return lax.psum(backward, "tok") * factor

    def totals(values):
        return lax.psum(values, "feat")

    image_x = project(current_block.astype(jnp.bfloat16))
    rayleigh = totals(jnp.dot(current_block.T, image_x, precision=highest))
    residual = image_x - jnp.dot(current_block, rayleigh, precision=highest)
    lengths = totals(jnp.sum(residual * residual, axis=0, keepdims=True))
    unit_residual = residual * lax.rsqrt(lengths + 1e-06)
    residual_half = unit_residual.astype(jnp.bfloat16)
    trailing = project(jnp.concatenate([residual_half, directions.astype(jnp.bfloat16)], axis=1))
    image_r = trailing[:, :block_cols]
    image_p = trailing[:, block_cols:]
    image_local = jnp.concatenate([image_x, image_r, image_p], axis=1)
    search = jnp.concatenate([current_block, unit_residual, directions], axis=1)
    gram_image, gram_search = totals(
        (
            jnp.dot(search.T, image_local, precision=highest),
            jnp.dot(search.T, search, precision=highest),
        )
    )
    return (image_local, gram_image, gram_search)


MESH = pl.DeviceIdType.MESH
NT = (((1,), (1,)), ((), ()))
TN = (((0,), (0,)), ((), ()))
GROUP = 4


def step_kernel(tok_count_all, factor, h_ref, xt_ref, pt_ref, img_ref, gram_ref, h_buf, search, vecs_xp, vecs_r,
                part_xp, got_xp, part_r, got_r, proj_xp, proj_r, halo_tx_xp, halo_rx_xp, halo_tx_r, halo_rx_r,
                lag_xp, lag_r, tx1, rx1, own1, tx2, rx2, own2, gathered, small_tx, small_rx, gram_tx, gram_rx,
                h_sem, feat_s, feat_r, halo_s, halo_r, one_s, one_r, two_s, two_r, up_s, up_r, out_s, out_r,
                small_s, small_r):
    rows, depth = h_buf.shape
    k = xt_ref.shape[0]
    tok, feat = lax.axis_index("tok"), lax.axis_index("feat")
    low, high = lax.rem(tok, GROUP), lax.div(tok, GROUP)
    levels = tok_count_all // GROUP
    block, piece = depth // GROUP, depth // tok_count_all
    chunk = rows // 4
    order = (0, 3, 1, 2)
    highest = lax.Precision.HIGHEST

    def low_peer(s):
        return (high * GROUP + lax.rem(low + s, GROUP), feat)

    def high_peer(s):
        return (lax.rem(high + s, levels) * GROUP + low, feat)

    other = (tok, 1 - feat)
    after = (lax.rem(tok + 1, tok_count_all), feat)
    before = (lax.rem(tok + tok_count_all - 1, tok_count_all), feat)

    loads = {}
    for c in order:
        part = pl.ds(c * chunk, chunk)
        loads[c] = pltpu.make_async_copy(h_ref.at[part], h_buf.at[part], h_sem.at[c])
        loads[c].start()

    peers = [other, after, before] + [low_peer(s) for s in range(1, GROUP)] + [high_peer(s) for s in range(1, levels)]
    barrier = pltpu.get_barrier_semaphore()
    for peer in peers:
        pl.semaphore_signal(barrier, inc=1, device_id=peer, device_id_type=MESH)

    search[0:k] = xt_ref[...]
    search[2 * k : 3 * k] = pt_ref[...]
    vecs_xp[0:k] = xt_ref[...].astype(jnp.bfloat16)
    vecs_xp[k : 2 * k] = pt_ref[...].astype(jnp.bfloat16)
    pl.semaphore_wait(barrier, len(peers))
    sent = []

    def send(src, dst, s_sem, r_sem, peer):
        copy = pltpu.make_async_remote_copy(
            src_ref=src, dst_ref=dst, send_sem=s_sem, recv_sem=r_sem, device_id=peer, device_id_type=MESH
        )
        copy.start()
        sent.append(copy)
        return copy

    def project(at, vecs, part, got, proj, halo_tx, halo_rx, lag, between):
        copies = {}
        for c in order:
            span = pl.ds(c * chunk, chunk)
            if at == 0:
                loads[c].wait()
            part[span] = lax.dot_general(h_buf[span], vecs[...], NT, preferred_element_type=jnp.float32)
            copies[c] = send(part.at[span], got.at[span], feat_s.at[at, c], feat_r.at[at, c], other)
        between()
        halos = []
        for c in order:
            span = pl.ds(c * chunk, chunk)
            copies[c].wait_recv()
            proj[span] = part[span] + got[span]
            if c == 0:
                halo_tx[0] = proj[0:LAG].astype(jnp.bfloat16)
                halos.append(send(halo_tx.at[0], halo_rx.at[0], halo_s.at[at, 0], halo_r.at[at, 0], before))
            if c == 3:
                halo_tx[1] = proj[rows - LAG : rows].astype(jnp.bfloat16)
                halos.append(send(halo_tx.at[1], halo_rx.at[1], halo_s.at[at, 1], halo_r.at[at, 1], after))
        lag[LAG : rows - LAG] = (proj[2 * LAG : rows] + proj[0 : rows - 2 * LAG]).astype(jnp.bfloat16)
        for copy in halos:
            copy.wait_recv()
        ahead = jnp.where(tok == tok_count_all - 1, 0.0, halo_rx[0].astype(jnp.float32))
        behind = jnp.where(tok == 0, 0.0, halo_rx[1].astype(jnp.float32))
        lag[0:LAG] = (proj[LAG : 2 * LAG] + behind).astype(jnp.bfloat16)
        lag[rows - LAG : rows] = (ahead + proj[rows - 2 * LAG : rows - LAG]).astype(jnp.bfloat16)

    def backward(lag, s):
        at = pl.multiple_of(lax.rem(low + s, GROUP) * block, block)
        return lax.dot_general(lag[...], h_buf[:, pl.ds(at, block)], TN, preferred_element_type=jnp.float32)

    def send_one(n, s):
        return send(tx1.at[n, s - 1], rx1.at[n, s - 1], one_s.at[n, s - 1], one_r.at[n, s - 1], low_peer(s))

    def level_two(n, first):
        for copy in first:
            copy.wait_recv()
        total = own1[n]
        for s in range(1, GROUP):
            total = total + rx1[n, s - 1].astype(jnp.float32)
        own1[n] = total
        copies = []
        for s in range(1, levels):
            at = pl.multiple_of(lax.rem(high + s, levels) * piece, piece)
            tx2[n, s - 1] = own1[n, :, pl.ds(at, piece)].astype(jnp.bfloat16)
            copies.append(
                send(tx2.at[n, s - 1], rx2.at[n, s - 1], two_s.at[n, s - 1], two_r.at[n, s - 1], high_peer(s))
            )
        return copies

    def spot(h):
        return pl.ds(pl.multiple_of(low * block + h * piece, piece), piece)

    def outward(n, e):
        h = lax.rem(high + levels - e, levels)
        view = gathered.at[n, :, spot(h)]
        return [
            send(view, view, out_s.at[n, e, s - 1], out_r.at[n, e, s - 1], low_peer(s)) for s in range(1, GROUP)
        ]

    def finish(n, second):
        for copy in second:
            copy.wait_recv()
        at = pl.multiple_of(high * piece, piece)
        total = own1[n, :, pl.ds(at, piece)]
        for s in range(1, levels):
            total = total + rx2[n, s - 1].astype(jnp.float32)
        gathered[n, :, spot(high)] = (total * factor).astype(jnp.bfloat16)
        view = gathered.at[n, :, spot(high)]
        ups = [send(view, view, up_s.at[n, s - 1], up_r.at[n, s - 1], high_peer(s)) for s in range(1, levels)]
        return ups, outward(n, 0)

    def forward(n, ups):
        outs = []
        for e in range(1, levels):
            ups[e - 1].wait_recv()
            outs += outward(n, e)
        return outs

    def arrive(n, outs):
        for copy in outs:
            copy.wait_recv()
        value = gathered[n].astype(jnp.float32)
        img_ref[n * k : (n + 1) * k] = value
        return value

    project(0, vecs_xp, part_xp, got_xp, proj_xp, halo_tx_xp, halo_rx_xp, lag_xp, lambda: None)
    first_x = []
    for s in (1, 2, 3, 0):
        both = backward(lag_xp, s)
        if s == 0:
            own1[0] = both[0:k]
            own1[2] = both[k : 2 * k]
        else:
            tx1[0, s - 1] = both[0:k].astype(jnp.bfloat16)
            tx1[2, s - 1] = both[k : 2 * k].astype(jnp.bfloat16)
            first_x.append(send_one(0, s))
    second_x = level_two(0, first_x)
    ups_x, outs_x = finish(0, second_x)
    outs_x += forward(0, ups_x)
    first_p = [send_one(2, s) for s in (1, 2, 3)]
    image = arrive(0, outs_x)

    small_tx[0] = lax.dot_general(image, search[0:k], NT, precision=highest, preferred_element_type=jnp.float32)
    copy = send(small_tx.at[0], small_rx.at[0], small_s.at[0], small_r.at[0], other)
    second_p = level_two(2, first_p)
    copy.wait_recv()
    rayleigh_t = small_tx[0] + small_rx[0]
    residual = img_ref[0:k] - jnp.dot(
        rayleigh_t, search[0:k], precision=highest, preferred_element_type=jnp.float32
    )
    search[k : 2 * k] = residual
    small_tx[1] = jnp.broadcast_to(jnp.sum(residual * residual, axis=1, keepdims=True), (k, k))
    copy = send(small_tx.at[1], small_rx.at[1], small_s.at[1], small_r.at[1], other)
    ups_p, outs_p = finish(2, second_p)
    copy.wait_recv()
    lengths = (small_tx[1] + small_rx[1])[:, 0:1]
    unit = search[k : 2 * k] * lax.rsqrt(lengths + 1e-06)
    search[k : 2 * k] = unit
    vecs_r[...] = unit.astype(jnp.bfloat16)

    outs_more = []

    def between():
        outs_more.extend(forward(2, ups_p))

    project(1, vecs_r, part_r, got_r, proj_r, halo_tx_r, halo_rx_r, lag_r, between)
    first_r = []
    for s in (1, 2, 3, 0):
        value = backward(lag_r, s)
        if s == 0:
            own1[1] = value
        else:
            tx1[1, s - 1] = value.astype(jnp.bfloat16)
            first_r.append(send_one(1, s))

    def gram(row, left):
        gram_tx[row : row + k] = lax.dot_general(
            left, search[...], NT, precision=highest, preferred_element_type=jnp.float32
        )

    second_r = level_two(1, first_r)
    arrive(2, outs_p + outs_more)
    gram(k, img_ref[0:k])
    ups_r, outs_r = finish(1, second_r)
    outs_r += forward(1, ups_r)
    gram(2 * k, img_ref[2 * k : 3 * k])
    for b in range(3):
        gram((3 + b) * k, search[b * k : (b + 1) * k])
    rest = pl.ds(k, 5 * k)
    copy_rest = send(gram_tx.at[rest], gram_rx.at[rest], small_s.at[2], small_r.at[2], other)
    arrive(1, outs_r)
    gram(0, img_ref[k : 2 * k])
    last = pl.ds(0, k)
    copy_last = send(gram_tx.at[last], gram_rx.at[last], small_s.at[3], small_r.at[3], other)
    copy_rest.wait_recv()
    gram_ref[0:k] = gram_tx[k : 2 * k] + gram_rx[k : 2 * k]
    gram_ref[2 * k : 6 * k] = gram_tx[2 * k : 6 * k] + gram_rx[2 * k : 6 * k]
    copy_last.wait_recv()
    gram_ref[k : 2 * k] = gram_tx[0:k] + gram_rx[0:k]
    for copy in sent:
        copy.wait_send()


def local_kernel(hidden_states, current_block, directions):
    rows, depth = hidden_states.shape
    k = current_block.shape[1]
    count = lax.axis_size("tok")
    levels = count // GROUP
    factor = 0.5 / math.sqrt(rows * count - LAG)
    block, piece = depth // GROUP, depth // count
    f32, bf16 = jnp.float32, jnp.bfloat16
    vmem = pl.BlockSpec(memory_space=pltpu.VMEM)
    dma = pltpu.SemaphoreType.DMA
    scratch = [
        pltpu.VMEM((rows, depth), bf16),
        pltpu.VMEM((3 * k, depth), f32),
        pltpu.VMEM((2 * k, depth), bf16),
        pltpu.VMEM((k, depth), bf16),
        pltpu.VMEM((rows, 2 * k), f32),
        pltpu.VMEM((rows, 2 * k), f32),
        pltpu.VMEM((rows, k), f32),
        pltpu.VMEM((rows, k), f32),
        pltpu.VMEM((rows, 2 * k), f32),
        pltpu.VMEM((rows, k), f32),
        pltpu.VMEM((2, LAG, 2 * k), bf16),
        pltpu.VMEM((2, LAG, 2 * k), bf16),
        pltpu.VMEM((2, LAG, k), bf16),
        pltpu.VMEM((2, LAG, k), bf16),
        pltpu.VMEM((rows, 2 * k), bf16),
        pltpu.VMEM((rows, k), bf16),
        pltpu.VMEM((3, GROUP - 1, k, block), bf16),
        pltpu.VMEM((3, GROUP - 1, k, block), bf16),
        pltpu.VMEM((3, k, block), f32),
        pltpu.VMEM((3, levels - 1, k, piece), bf16),
        pltpu.VMEM((3, levels - 1, k, piece), bf16),
        pltpu.VMEM((3, k, piece), f32),
        pltpu.VMEM((3, k, depth), bf16),
        pltpu.VMEM((2, k, k), f32),
        pltpu.VMEM((2, k, k), f32),
        pltpu.VMEM((6 * k, 3 * k), f32),
        pltpu.VMEM((6 * k, 3 * k), f32),
        dma((4,)),
        dma((2, 4)), dma((2, 4)),
        dma((2, 2)), dma((2, 2)),
        dma((3, GROUP - 1)), dma((3, GROUP - 1)),
        dma((3, levels - 1)), dma((3, levels - 1)),
        dma((3, levels - 1)), dma((3, levels - 1)),
        dma((3, levels, GROUP - 1)), dma((3, levels, GROUP - 1)),
        dma((4,)), dma((4,)),
    ]
    image_t, grams = pl.pallas_call(
        functools.partial(step_kernel, count, factor),
        out_shape=(jax.ShapeDtypeStruct((3 * k, depth), f32), jax.ShapeDtypeStruct((6 * k, 3 * k), f32)),
        in_specs=[pl.BlockSpec(memory_space=pl.ANY), vmem, vmem],
        out_specs=(vmem, vmem),
        scratch_shapes=scratch,
        compiler_params=pltpu.CompilerParams(
            collective_id=0, has_side_effects=True, vmem_limit_bytes=56 * 1024 * 1024
        ),
        cost_estimate=pl.CostEstimate(
            flops=12 * rows * depth * k, bytes_accessed=2 * rows * depth, transcendentals=0
        ),
        name="lobpcg_step",
    )(hidden_states, current_block.T, directions.T)
    return image_t.T, grams[: 3 * k].T, grams[3 * k :]


def solution(mesh):
    def program(hidden_states, current_block, directions):
        count, halves = mesh.shape["tok"], mesh.shape["feat"]
        depth = hidden_states.shape[1] // halves
        whole_tiles = count % GROUP == 0 and count > GROUP and depth % (128 * count) == 0
        return jax.shard_map(
            local_kernel if halves == 2 and whole_tiles else local,
            mesh=mesh,
            in_specs=(P("tok", "feat"), P("feat", None), P("feat", None)),
            out_specs=(P("feat", None), P(), P()),
            check_vma=False,
        )(hidden_states, current_block, directions)

    return program
```

```python
import functools
import math

import jax
import jax.numpy as jnp
from jax import lax
from jax.experimental import pallas as pl
from jax.experimental.pallas import tpu as pltpu
from jax.sharding import PartitionSpec as P

LAG = 256


def extended(value, sides, width):
    for axis, dim in sides:
        count, length = (lax.axis_size(axis), value.shape[dim])
        up = [(i, (i + 1) % count) for i in range(count - 1)]
        down = [(j, i) for i, j in up]
        last = lax.slice_in_dim(value, length - width, length, axis=dim)
        initial = lax.slice_in_dim(value, 0, width, axis=dim)
        before = lax.ppermute(last, axis, up)
        after = lax.ppermute(initial, axis, down)
        value = jnp.concatenate([before, value, after], axis=dim)
    return value


def local(hidden_states, current_block, directions):
    highest = lax.Precision.HIGHEST
    tok_count = hidden_states.shape[0]
    block_cols = current_block.shape[1]
    tokens_all = tok_count * lax.axis_size("tok")
    factor = 0.5 / math.sqrt(tokens_all - LAG)

    def project(vectors):
        partial_value = jnp.dot(hidden_states, vectors, preferred_element_type=jnp.float32)
        projected = lax.psum(partial_value, "feat")
        padded = extended(projected, (("tok", 0),), LAG)
        lagged = (padded[2 * LAG : 2 * LAG + tok_count] + padded[:tok_count]).astype(jnp.bfloat16)
        backward = lax.dot_general(
            hidden_states, lagged, (((0,), (0,)), ((), ())), preferred_element_type=jnp.float32
        )
        return lax.psum(backward, "tok") * factor

    def totals(values):
        return lax.psum(values, "feat")

    image_x = project(current_block.astype(jnp.bfloat16))
    rayleigh = totals(jnp.dot(current_block.T, image_x, precision=highest))
    residual = image_x - jnp.dot(current_block, rayleigh, precision=highest)
    lengths = totals(jnp.sum(residual * residual, axis=0, keepdims=True))
    unit_residual = residual * lax.rsqrt(lengths + 1e-06)
    residual_half = unit_residual.astype(jnp.bfloat16)
    trailing = project(jnp.concatenate([residual_half, directions.astype(jnp.bfloat16)], axis=1))
    image_r = trailing[:, :block_cols]
    image_p = trailing[:, block_cols:]
    image_local = jnp.concatenate([image_x, image_r, image_p], axis=1)
    search = jnp.concatenate([current_block, unit_residual, directions], axis=1)
    gram_image, gram_search = totals(
        (
            jnp.dot(search.T, image_local, precision=highest),
            jnp.dot(search.T, search, precision=highest),
        )
    )
    return (image_local, gram_image, gram_search)


MESH = pl.DeviceIdType.MESH
NT = (((1,), (1,)), ((), ()))
TN = (((0,), (0,)), ((), ()))
GROUP = 4


def step_kernel(tok_count_all, factor, h_ref, xt_ref, pt_ref, img_ref, gram_ref, h_buf, search, resid,
                part_xp, got_xp, part_r, got_r, proj_xp, proj_r, halo_tx_xp, halo_rx_xp, halo_tx_r, halo_rx_r,
                lag_xp, lag_r, lag_t, tx1, rx1, own1, tx2, rx2, gathered, small_tx, small_rx,
                gxp_tx, gxp_rx, gr_tx, gr_rx, gs_tx, gs_rx,
                h_sem, feat_s, feat_r, halo_s, halo_r, one_s, one_r, two_s, two_r, up_s, up_r, out_s, out_r,
                small_s, small_r):
    rows, depth = h_buf.shape
    k = xt_ref.shape[0]
    tok, feat = lax.axis_index("tok"), lax.axis_index("feat")
    low, high = lax.rem(tok, GROUP), lax.div(tok, GROUP)
    levels = tok_count_all // GROUP
    block, piece = depth // GROUP, depth // tok_count_all
    chunk = rows // 4
    order = (0, 3, 1, 2)
    near = tuple(range(1, GROUP))
    far = tuple(range(1, levels))
    f32, bf16 = jnp.float32, jnp.bfloat16

    def low_peer(s):
        return (high * GROUP + lax.rem(low + s, GROUP), feat)

    def high_peer(s):
        return (lax.rem(high + s, levels) * GROUP + low, feat)

    other = (tok, 1 - feat)
    after = (lax.rem(tok + 1, tok_count_all), feat)
    before = (lax.rem(tok + tok_count_all - 1, tok_count_all), feat)

    loads = {}
    for c in order:
        part = pl.ds(c * chunk, chunk)
        loads[c] = pltpu.make_async_copy(h_ref.at[part], h_buf.at[part], h_sem.at[c])
        loads[c].start()

    peers = [other, after, before] + [low_peer(s) for s in near] + [high_peer(s) for s in far]
    barrier = pltpu.get_barrier_semaphore()
    for peer in peers:
        pl.semaphore_signal(barrier, inc=1, device_id=peer, device_id_type=MESH)

    def split(n, value):
        rounded = value.astype(bf16)
        search[n * k : (n + 1) * k] = rounded
        search[(3 + n) * k : (4 + n) * k] = (value - rounded.astype(f32)).astype(bf16)

    split(0, xt_ref[...])
    split(1, pt_ref[...])
    pl.semaphore_wait(barrier, len(peers))
    sent = []

    def send(src, dst, s_sem, r_sem, peer):
        copy = pltpu.make_async_remote_copy(
            src_ref=src, dst_ref=dst, send_sem=s_sem, recv_sem=r_sem, device_id=peer, device_id_type=MESH
        )
        copy.start()
        sent.append(copy)
        return copy

    def nt(left, right):
        return lax.dot_general(left, right, NT, preferred_element_type=f32)

    def dot(left, right):
        return jnp.dot(left, right, preferred_element_type=f32)

    def project(at, vecs, part, got, proj, halo_tx, halo_rx, lag, between):
        copies = {}
        for c in order:
            span = pl.ds(c * chunk, chunk)
            if at == 0:
                loads[c].wait()
            part[span] = nt(h_buf[span], vecs)
            copies[c] = send(part.at[span], got.at[span], feat_s.at[at, c], feat_r.at[at, c], other)
        halos = []
        for c in order:
            span = pl.ds(c * chunk, chunk)
            copies[c].wait_recv()
            proj[span] = part[span] + got[span]
            if c == 0:
                halo_tx[0] = proj[0:LAG].astype(bf16)
                halos.append(send(halo_tx.at[0], halo_rx.at[0], halo_s.at[at, 0], halo_r.at[at, 0], before))
            if c == 3:
                halo_tx[1] = proj[rows - LAG : rows].astype(bf16)
                halos.append(send(halo_tx.at[1], halo_rx.at[1], halo_s.at[at, 1], halo_r.at[at, 1], after))
        lag[LAG : rows - LAG] = proj[2 * LAG : rows] + proj[0 : rows - 2 * LAG]
        between()
        for copy in halos:
            copy.wait_recv()
        ahead = jnp.where(tok == tok_count_all - 1, 0.0, halo_rx[0].astype(f32))
        behind = jnp.where(tok == 0, 0.0, halo_rx[1].astype(f32))
        lag[0:LAG] = proj[LAG : 2 * LAG] + behind
        lag[rows - LAG : rows] = ahead + proj[rows - 2 * LAG : rows - LAG]
        lag_t[0 : lag.shape[1]] = lag[...].T.astype(bf16)

    def lanes(j, h):
        return pl.ds(pl.multiple_of(j * block + h * piece, piece), piece)

    def backward(width, s, e):
        spot = lanes(lax.rem(low + s, GROUP), lax.rem(high + e, levels))
        return dot(lag_t[0:width], h_buf[:, spot])

    def send_one(n, s, e):
        at = (n, s - 1, e)
        return send(tx1.at[at], rx1.at[at], one_s.at[at], one_r.at[at], low_peer(s))

    def reduce_one(n, e, first):
        for copy in first:
            copy.wait_recv()
        total = own1[n, e]
        for s in near:
            total = total + rx1[n, s - 1, e].astype(f32)
        return total

    def level_two(n, e, first):
        tx2[n, e - 1] = reduce_one(n, e, first).astype(bf16)
        at = (n, e - 1)
        return send(tx2.at[at], rx2.at[at], two_s.at[at], two_r.at[at], high_peer(e))

    def outward(n, e):
        view = gathered.at[pl.ds(n * k, k), lanes(low, lax.rem(high + levels - e, levels))]
        return [send(view, view, out_s.at[n, e, s - 1], out_r.at[n, e, s - 1], low_peer(s)) for s in near]

    def finish(n, first, second):
        total = reduce_one(n, 0, first)
        for s in far:
            second[s - 1].wait_recv()
            total = total + rx2[n, s - 1].astype(f32)
        spot = lanes(low, high)
        gathered[n * k : (n + 1) * k, spot] = (total * factor).astype(bf16)
        view = gathered.at[pl.ds(n * k, k), spot]
        ups = [send(view, view, up_s.at[n, s - 1], up_r.at[n, s - 1], high_peer(s)) for s in far]
        return ups, outward(n, 0)

    def forward(n, ups):
        outs = []
        for e in far:
            ups[e - 1].wait_recv()
            outs += outward(n, e)
        return outs

    def arrive(n, outs, place):
        for copy in outs:
            copy.wait_recv()
        img_ref[place * k : (place + 1) * k] = gathered[n * k : (n + 1) * k].astype(f32)

    def products(n, extra):
        width = k if extra is None else 2 * k
        first, second = {}, []
        steps = far + (0,)
        for i, e in enumerate(steps):
            first[e] = []
            for s in near + (0,):
                value = backward(width, s, e)
                for m in (n,) if extra is None else (n, extra):
                    own = value[0:k] if m == n else value[k : 2 * k]
                    if s == 0:
                        own1[m, e] = own
                    else:
                        tx1[m, s - 1, e] = own.astype(bf16)
                if s != 0:
                    first[e].append(send_one(n, s, e))
            if i > 0:
                second.append(level_two(n, steps[i - 1], first[steps[i - 1]]))
        return first[0], second

    project(0, search[0 : 2 * k], part_xp, got_xp, proj_xp, halo_tx_xp, halo_rx_xp, lag_xp, lambda: None)
    first_x, second_x = products(0, 1)
    ups_x, outs_x = finish(0, first_x, second_x)
    outs_x += forward(0, ups_x)
    first_p = {e: [send_one(1, s, e) for s in near] for e in far + (0,)}
    arrive(0, outs_x, 0)

    image = gathered[0:k]
    small_tx[0] = nt(image, search[0:k]) + nt(image, search[3 * k : 4 * k])
    copy = send(small_tx.at[0], small_rx.at[0], small_s.at[0], small_r.at[0], other)
    second_p = [level_two(1, e, first_p[e]) for e in far]
    copy.wait_recv()
    rayleigh_t = small_tx[0] + small_rx[0]
    upper = rayleigh_t.astype(bf16)
    under = (rayleigh_t - upper.astype(f32)).astype(bf16)
    main, rest = search[0:k], search[3 * k : 4 * k]
    residual = img_ref[0:k] - (dot(upper, main) + (dot(under, main) + dot(upper, rest)))
    resid[...] = residual
    small_tx[1] = jnp.broadcast_to(jnp.sum(residual * residual, axis=1, keepdims=True), (k, k))
    copy = send(small_tx.at[1], small_rx.at[1], small_s.at[1], small_r.at[1], other)
    ups_p, outs_p = finish(1, first_p[0], second_p)
    copy.wait_recv()
    lengths = (small_tx[1] + small_rx[1])[:, 0:1]
    split(2, resid[...] * lax.rsqrt(lengths + 1e-06))

    def between():
        outs_p.extend(forward(1, ups_p))

    project(1, search[2 * k : 3 * k], part_r, got_r, proj_r, halo_tx_r, halo_rx_r, lag_r, between)
    first_r, second_r = products(2, None)
    ups_r, outs_r = finish(2, first_r, second_r)
    outs_r += forward(2, ups_r)

    def exchange(at, tx, rx):
        return send(tx, rx, small_s.at[at], small_r.at[at], other)

    arrive(1, outs_p, 2)
    both = nt(search[...], gathered[0 : 2 * k])
    gxp_tx[...] = both[0 : 3 * k] + both[3 * k : 6 * k]
    copy_xp = exchange(2, gxp_tx, gxp_rx)
    main = search[0 : 3 * k]
    both = nt(search[...], main)
    gs_tx[...] = both[0 : 3 * k] + (both[3 * k : 6 * k] + nt(main, search[3 * k : 6 * k]))
    copy_gs = exchange(3, gs_tx, gs_rx)
    arrive(2, outs_r, 1)
    both = nt(search[...], gathered[2 * k : 3 * k])
    gr_tx[...] = both[0 : 3 * k] + both[3 * k : 6 * k]
    copy_gr = exchange(4, gr_tx, gr_rx)
    places = (0, 2, 1)
    copy_gs.wait_recv()
    copy_xp.wait_recv()
    squares = gs_tx[...] + gs_rx[...]
    sides = gxp_tx[...] + gxp_rx[...]
    copy_gr.wait_recv()
    middle = gr_tx[...] + gr_rx[...]
    images = jnp.concatenate([sides[:, 0:k], middle, sides[:, k : 2 * k]], axis=1)
    squares = jnp.concatenate([squares[:, 0:k], squares[:, 2 * k : 3 * k], squares[:, k : 2 * k]], axis=1)
    for n, place in enumerate(places):
        gram_ref[0, place * k : (place + 1) * k] = images[n * k : (n + 1) * k]
        gram_ref[1, place * k : (place + 1) * k] = squares[n * k : (n + 1) * k]
    for copy in sent:
        copy.wait_send()


def local_kernel(hidden_states, current_block, directions):
    rows, depth = hidden_states.shape
    k = current_block.shape[1]
    count = lax.axis_size("tok")
    levels = count // GROUP
    factor = 0.5 / math.sqrt(rows * count - LAG)
    piece = depth // count
    f32, bf16 = jnp.float32, jnp.bfloat16
    vmem = pl.BlockSpec(memory_space=pltpu.VMEM)
    dma = pltpu.SemaphoreType.DMA
    scratch = [
        pltpu.VMEM((rows, depth), bf16),
        pltpu.VMEM((6 * k, depth), bf16),
        pltpu.VMEM((k, depth), f32),
        pltpu.VMEM((rows, 2 * k), f32),
        pltpu.VMEM((rows, 2 * k), f32),
        pltpu.VMEM((rows, k), f32),
        pltpu.VMEM((rows, k), f32),
        pltpu.VMEM((rows, 2 * k), f32),
        pltpu.VMEM((rows, k), f32),
        pltpu.VMEM((2, LAG, 2 * k), bf16),
        pltpu.VMEM((2, LAG, 2 * k), bf16),
        pltpu.VMEM((2, LAG, k), bf16),
        pltpu.VMEM((2, LAG, k), bf16),
        pltpu.VMEM((rows, 2 * k), f32),
        pltpu.VMEM((rows, k), f32),
        pltpu.VMEM((2 * k, rows), bf16),
        pltpu.VMEM((3, GROUP - 1, levels, k, piece), bf16),
        pltpu.VMEM((3, GROUP - 1, levels, k, piece), bf16),
        pltpu.VMEM((3, levels, k, piece), f32),
        pltpu.VMEM((3, levels - 1, k, piece), bf16),
        pltpu.VMEM((3, levels - 1, k, piece), bf16),
        pltpu.VMEM((3 * k, depth), bf16),
        pltpu.VMEM((2, k, k), f32),
        pltpu.VMEM((2, k, k), f32),
        pltpu.VMEM((3 * k, 2 * k), f32),
        pltpu.VMEM((3 * k, 2 * k), f32),
        pltpu.VMEM((3 * k, k), f32),
        pltpu.VMEM((3 * k, k), f32),
        pltpu.VMEM((3 * k, 3 * k), f32),
        pltpu.VMEM((3 * k, 3 * k), f32),
        dma((4,)),
        dma((2, 4)), dma((2, 4)),
        dma((2, 2)), dma((2, 2)),
        dma((3, GROUP - 1, levels)), dma((3, GROUP - 1, levels)),
        dma((3, levels - 1)), dma((3, levels - 1)),
        dma((3, levels - 1)), dma((3, levels - 1)),
        dma((3, levels, GROUP - 1)), dma((3, levels, GROUP - 1)),
        dma((5,)), dma((5,)),
    ]
    image_t, grams = pl.pallas_call(
        functools.partial(step_kernel, count, factor),
        out_shape=(jax.ShapeDtypeStruct((3 * k, depth), f32), jax.ShapeDtypeStruct((2, 3 * k, 3 * k), f32)),
        in_specs=[pl.BlockSpec(memory_space=pl.ANY), vmem, vmem],
        out_specs=(vmem, vmem),
        scratch_shapes=scratch,
        compiler_params=pltpu.CompilerParams(
            collective_id=0, has_side_effects=True, vmem_limit_bytes=56 * 1024 * 1024
        ),
        cost_estimate=pl.CostEstimate(
            flops=12 * rows * depth * k, bytes_accessed=2 * rows * depth, transcendentals=0
        ),
        name="lobpcg_step",
    )(hidden_states, current_block.T, directions.T)
    return image_t.T, grams[0], grams[1]


def solution(mesh):
    def program(hidden_states, current_block, directions):
        count, halves = mesh.shape["tok"], mesh.shape["feat"]
        depth = hidden_states.shape[1] // halves
        whole_tiles = count % GROUP == 0 and count > GROUP and depth % (128 * count) == 0
        return jax.shard_map(
            local_kernel if halves == 2 and whole_tiles else local,
            mesh=mesh,
            in_specs=(P("tok", "feat"), P("feat", None), P("feat", None)),
            out_specs=(P("feat", None), P(), P()),
            check_vma=False,
        )(hidden_states, current_block, directions)

    return program
```

```python
import functools
import math

import jax
import jax.numpy as jnp
from jax import lax
from jax.experimental import pallas as pl
from jax.experimental.pallas import tpu as pltpu
from jax.sharding import PartitionSpec as P

LAG = 256


def extended(value, sides, width):
    for axis, dim in sides:
        count, length = (lax.axis_size(axis), value.shape[dim])
        up = [(i, (i + 1) % count) for i in range(count - 1)]
        down = [(j, i) for i, j in up]
        last = lax.slice_in_dim(value, length - width, length, axis=dim)
        initial = lax.slice_in_dim(value, 0, width, axis=dim)
        before = lax.ppermute(last, axis, up)
        after = lax.ppermute(initial, axis, down)
        value = jnp.concatenate([before, value, after], axis=dim)
    return value


def local(hidden_states, current_block, directions):
    highest = lax.Precision.HIGHEST
    tok_count = hidden_states.shape[0]
    block_cols = current_block.shape[1]
    tokens_all = tok_count * lax.axis_size("tok")
    factor = 0.5 / math.sqrt(tokens_all - LAG)

    def project(vectors):
        partial_value = jnp.dot(hidden_states, vectors, preferred_element_type=jnp.float32)
        projected = lax.psum(partial_value, "feat")
        padded = extended(projected, (("tok", 0),), LAG)
        lagged = (padded[2 * LAG : 2 * LAG + tok_count] + padded[:tok_count]).astype(jnp.bfloat16)
        backward = lax.dot_general(
            hidden_states, lagged, (((0,), (0,)), ((), ())), preferred_element_type=jnp.float32
        )
        return lax.psum(backward, "tok") * factor

    def totals(values):
        return lax.psum(values, "feat")

    image_x = project(current_block.astype(jnp.bfloat16))
    rayleigh = totals(jnp.dot(current_block.T, image_x, precision=highest))
    residual = image_x - jnp.dot(current_block, rayleigh, precision=highest)
    lengths = totals(jnp.sum(residual * residual, axis=0, keepdims=True))
    unit_residual = residual * lax.rsqrt(lengths + 1e-06)
    residual_half = unit_residual.astype(jnp.bfloat16)
    trailing = project(jnp.concatenate([residual_half, directions.astype(jnp.bfloat16)], axis=1))
    image_r = trailing[:, :block_cols]
    image_p = trailing[:, block_cols:]
    image_local = jnp.concatenate([image_x, image_r, image_p], axis=1)
    search = jnp.concatenate([current_block, unit_residual, directions], axis=1)
    gram_image, gram_search = totals(
        (
            jnp.dot(search.T, image_local, precision=highest),
            jnp.dot(search.T, search, precision=highest),
        )
    )
    return (image_local, gram_image, gram_search)


MESH = pl.DeviceIdType.MESH
NT = (((1,), (1,)), ((), ()))
TN = (((0,), (0,)), ((), ()))
GROUP = 4


def step_kernel(tok_count_all, factor, h_ref, xt_ref, pt_ref, img_ref, gram_ref, h_buf, search, resid,
                part_xp, got_xp, part_r, got_r, proj_xp, proj_r, halo_tx_xp, halo_rx_xp, halo_tx_r, halo_rx_r,
                lag_xp, lag_r, lag_t, tx1, rx1, own1, tx2, rx2, gathered, small_tx, small_rx,
                gxp_tx, gxp_rx, gr_tx, gr_rx, gs_tx, gs_rx,
                h_sem, feat_s, feat_r, halo_s, halo_r, one_s, one_r, two_s, two_r, up_s, up_r, out_s, out_r,
                small_s, small_r, img_sem):
    rows, depth = h_buf.shape
    k = xt_ref.shape[0]
    tok, feat = lax.axis_index("tok"), lax.axis_index("feat")
    low, high = lax.rem(tok, GROUP), lax.div(tok, GROUP)
    levels = tok_count_all // GROUP
    block, piece = depth // GROUP, depth // tok_count_all
    chunk = rows // 4
    order = (0, 3, 1, 2)
    near = tuple(range(1, GROUP))
    far = tuple(range(1, levels))
    f32, bf16 = jnp.float32, jnp.bfloat16

    def low_peer(s):
        return (high * GROUP + lax.rem(low + s, GROUP), feat)

    def high_peer(s):
        return (lax.rem(high + s, levels) * GROUP + low, feat)

    other = (tok, 1 - feat)
    after = (lax.rem(tok + 1, tok_count_all), feat)
    before = (lax.rem(tok + tok_count_all - 1, tok_count_all), feat)

    loads = {}
    for c in order:
        part = pl.ds(c * chunk, chunk)
        loads[c] = pltpu.make_async_copy(h_ref.at[part], h_buf.at[part], h_sem.at[c])
        loads[c].start()

    peers = [other, after, before] + [low_peer(s) for s in near] + [high_peer(s) for s in far]
    barrier = pltpu.get_barrier_semaphore()
    for peer in peers:
        pl.semaphore_signal(barrier, inc=1, device_id=peer, device_id_type=MESH)

    def split(n, value):
        rounded = value.astype(bf16)
        search[n * k : (n + 1) * k] = rounded
        search[(3 + n) * k : (4 + n) * k] = (value - rounded.astype(f32)).astype(bf16)

    split(0, xt_ref[...])
    split(1, pt_ref[...])
    pl.semaphore_wait(barrier, len(peers))
    sent, written = [], []

    def send(src, dst, s_sem, r_sem, peer):
        copy = pltpu.make_async_remote_copy(
            src_ref=src, dst_ref=dst, send_sem=s_sem, recv_sem=r_sem, device_id=peer, device_id_type=MESH
        )
        copy.start()
        sent.append(copy)
        return copy

    def nt(left, right):
        return lax.dot_general(left, right, NT, preferred_element_type=f32)

    def dot(left, right):
        return jnp.dot(left, right, preferred_element_type=f32)

    def project(at, vecs, part, got, proj, halo_tx, halo_rx, lag, middle, between):
        copies = {}
        for c in order:
            span = pl.ds(c * chunk, chunk)
            if at == 0:
                loads[c].wait()
            part[span] = nt(h_buf[span], vecs)
            copies[c] = send(part.at[span], got.at[span], feat_s.at[at, c], feat_r.at[at, c], other)
        middle()
        halos = []
        for c in order:
            span = pl.ds(c * chunk, chunk)
            copies[c].wait_recv()
            proj[span] = part[span] + got[span]
            if c == 0:
                halo_tx[0] = proj[0:LAG].astype(bf16)
                halos.append(send(halo_tx.at[0], halo_rx.at[0], halo_s.at[at, 0], halo_r.at[at, 0], before))
            if c == 3:
                halo_tx[1] = proj[rows - LAG : rows].astype(bf16)
                halos.append(send(halo_tx.at[1], halo_rx.at[1], halo_s.at[at, 1], halo_r.at[at, 1], after))
        lag[LAG : rows - LAG] = proj[2 * LAG : rows] + proj[0 : rows - 2 * LAG]
        between()
        for copy in halos:
            copy.wait_recv()
        ahead = jnp.where(tok == tok_count_all - 1, 0.0, halo_rx[0].astype(f32))
        behind = jnp.where(tok == 0, 0.0, halo_rx[1].astype(f32))
        lag[0:LAG] = proj[LAG : 2 * LAG] + behind
        lag[rows - LAG : rows] = ahead + proj[rows - 2 * LAG : rows - LAG]
        lag_t[0 : lag.shape[1]] = lag[...].T.astype(bf16)

    def lanes(j, h):
        return pl.ds(pl.multiple_of(j * block + h * piece, piece), piece)

    def backward(width, s, e):
        spot = lanes(lax.rem(low + s, GROUP), lax.rem(high + e, levels))
        return dot(lag_t[0:width], h_buf[:, spot])

    def send_one(n, s, e):
        at = (n, s - 1, e)
        return send(tx1.at[at], rx1.at[at], one_s.at[at], one_r.at[at], low_peer(s))

    def send_whole(n, s):
        at = (n, s - 1)
        return send(tx1.at[at], rx1.at[at], one_s.at[n, s - 1, 0], one_r.at[n, s - 1, 0], low_peer(s))

    def reduce_one(n, e, first):
        for copy in first:
            copy.wait_recv()
        total = own1[n, e]
        for s in near:
            total = total + rx1[n, s - 1, e].astype(f32)
        return total

    def level_two(n, e, first):
        tx2[n, e - 1] = reduce_one(n, e, first).astype(bf16)
        at = (n, e - 1)
        return send(tx2.at[at], rx2.at[at], two_s.at[at], two_r.at[at], high_peer(e))

    def outward(n, e):
        view = gathered.at[pl.ds(n * k, k), lanes(low, lax.rem(high + levels - e, levels))]
        return [send(view, view, out_s.at[n, e, s - 1], out_r.at[n, e, s - 1], low_peer(s)) for s in near]

    def finish(n, first, second, out=True):
        total = reduce_one(n, 0, first)
        for s in far:
            second[s - 1].wait_recv()
            total = total + rx2[n, s - 1].astype(f32)
        spot = lanes(low, high)
        gathered[n * k : (n + 1) * k, spot] = (total * factor).astype(bf16)
        view = gathered.at[pl.ds(n * k, k), spot]
        ups = [send(view, view, up_s.at[n, s - 1], up_r.at[n, s - 1], high_peer(s)) for s in far]
        return ups, outward(n, 0) if out else []

    def forward(n, ups):
        outs = []
        for e in far:
            ups[e - 1].wait_recv()
            outs += outward(n, e)
        return outs

    def arrive(n, outs, place):
        for copy in outs:
            copy.wait_recv()
        copy = pltpu.make_async_copy(
            gathered.at[pl.ds(n * k, k)], img_ref.at[pl.ds(place * k, k)], img_sem.at[n]
        )
        copy.start()
        written.append(copy)

    def products(n, extra):
        width = k if extra is None else 2 * k
        first, second = {}, []
        steps = far + (0,)
        for i, e in enumerate(steps):
            first[e] = []
            for s in near + (0,):
                value = backward(width, s, e)
                for m in (n,) if extra is None else (n, extra):
                    own = value[0:k] if m == n else value[k : 2 * k]
                    if s == 0:
                        own1[m, e] = own
                    else:
                        tx1[m, s - 1, e] = own.astype(bf16)
                if s != 0:
                    first[e].append(send_one(n, s, e))
            if i > 0:
                second.append(level_two(n, steps[i - 1], first[steps[i - 1]]))
        return first[0], second

    project(0, search[0 : 2 * k], part_xp, got_xp, proj_xp, halo_tx_xp, halo_rx_xp, lag_xp, lambda: None, lambda: None)
    first_x, second_x = products(0, 1)
    ups_x, outs_x = finish(0, first_x, second_x)
    outs_x += forward(0, ups_x)
    first_p = [send_whole(1, s) for s in near]
    arrive(0, outs_x, 0)

    image = gathered[0:k]
    small_tx[0] = nt(image, search[0:k]) + nt(image, search[3 * k : 4 * k])
    copy = send(small_tx.at[0], small_rx.at[0], small_s.at[0], small_r.at[0], other)
    copy.wait_recv()
    rayleigh_t = small_tx[0] + small_rx[0]
    upper = rayleigh_t.astype(bf16)
    under = (rayleigh_t - upper.astype(f32)).astype(bf16)
    main, rest = search[0:k], search[3 * k : 4 * k]
    residual = image.astype(f32) - (dot(upper, main) + (dot(under, main) + dot(upper, rest)))
    resid[...] = residual
    small_tx[1] = jnp.broadcast_to(jnp.sum(residual * residual, axis=1, keepdims=True), (k, k))
    copy = send(small_tx.at[1], small_rx.at[1], small_s.at[1], small_r.at[1], other)
    for part in first_p:
        part.wait_recv()
    second_p = [level_two(1, e, ()) for e in far]
    copy.wait_recv()
    lengths = (small_tx[1] + small_rx[1])[:, 0:1]
    split(2, resid[...] * lax.rsqrt(lengths + 1e-06))

    ups_p, outs_p = [], []

    def middle_p():
        ups_p.extend(finish(1, (), second_p, False)[0])

    def between():
        for copy in ups_p:
            copy.wait_recv()
        view = gathered.at[pl.ds(k, k), pl.ds(pl.multiple_of(low * block, block), block)]
        outs_p.extend(send(view, view, out_s.at[1, 0, s - 1], out_r.at[1, 0, s - 1], low_peer(s)) for s in near)

    project(1, search[2 * k : 3 * k], part_r, got_r, proj_r, halo_tx_r, halo_rx_r, lag_r, middle_p, between)
    first_r, second_r = products(2, None)
    ups_r, outs_r = finish(2, first_r, second_r)
    outs_r += forward(2, ups_r)

    def exchange(at, tx, rx):
        return send(tx, rx, small_s.at[at], small_r.at[at], other)

    arrive(1, outs_p, 2)
    both = nt(search[...], gathered[0 : 2 * k])
    gxp_tx[...] = both[0 : 3 * k] + both[3 * k : 6 * k]
    copy_xp = exchange(2, gxp_tx, gxp_rx)
    main = search[0 : 3 * k]
    both = nt(search[...], main)
    gs_tx[...] = both[0 : 3 * k] + (both[3 * k : 6 * k] + nt(main, search[3 * k : 6 * k]))
    copy_gs = exchange(3, gs_tx, gs_rx)
    arrive(2, outs_r, 1)
    both = nt(search[...], gathered[2 * k : 3 * k])
    gr_tx[...] = both[0 : 3 * k] + both[3 * k : 6 * k]
    copy_gr = exchange(4, gr_tx, gr_rx)
    places = (0, 2, 1)
    copy_gs.wait_recv()
    copy_xp.wait_recv()
    squares = gs_tx[...] + gs_rx[...]
    sides = gxp_tx[...] + gxp_rx[...]
    copy_gr.wait_recv()
    middle = gr_tx[...] + gr_rx[...]
    images = jnp.concatenate([sides[:, 0:k], middle, sides[:, k : 2 * k]], axis=1)
    squares = jnp.concatenate([squares[:, 0:k], squares[:, 2 * k : 3 * k], squares[:, k : 2 * k]], axis=1)
    for n, place in enumerate(places):
        gram_ref[0, place * k : (place + 1) * k] = images[n * k : (n + 1) * k]
        gram_ref[1, place * k : (place + 1) * k] = squares[n * k : (n + 1) * k]
    for copy in sent:
        copy.wait_send()
    for copy in written:
        copy.wait()


def local_kernel(hidden_states, current_block, directions):
    rows, depth = hidden_states.shape
    k = current_block.shape[1]
    count = lax.axis_size("tok")
    levels = count // GROUP
    factor = 0.5 / math.sqrt(rows * count - LAG)
    piece = depth // count
    f32, bf16 = jnp.float32, jnp.bfloat16
    vmem = pl.BlockSpec(memory_space=pltpu.VMEM)
    dma = pltpu.SemaphoreType.DMA
    scratch = [
        pltpu.VMEM((rows, depth), bf16),
        pltpu.VMEM((6 * k, depth), bf16),
        pltpu.VMEM((k, depth), f32),
        pltpu.VMEM((rows, 2 * k), f32),
        pltpu.VMEM((rows, 2 * k), f32),
        pltpu.VMEM((rows, k), f32),
        pltpu.VMEM((rows, k), f32),
        pltpu.VMEM((rows, 2 * k), f32),
        pltpu.VMEM((rows, k), f32),
        pltpu.VMEM((2, LAG, 2 * k), bf16),
        pltpu.VMEM((2, LAG, 2 * k), bf16),
        pltpu.VMEM((2, LAG, k), bf16),
        pltpu.VMEM((2, LAG, k), bf16),
        pltpu.VMEM((rows, 2 * k), f32),
        pltpu.VMEM((rows, k), f32),
        pltpu.VMEM((2 * k, rows), bf16),
        pltpu.VMEM((3, GROUP - 1, levels, k, piece), bf16),
        pltpu.VMEM((3, GROUP - 1, levels, k, piece), bf16),
        pltpu.VMEM((3, levels, k, piece), f32),
        pltpu.VMEM((3, levels - 1, k, piece), bf16),
        pltpu.VMEM((3, levels - 1, k, piece), bf16),
        pltpu.VMEM((3 * k, depth), bf16),
        pltpu.VMEM((2, k, k), f32),
        pltpu.VMEM((2, k, k), f32),
        pltpu.VMEM((3 * k, 2 * k), f32),
        pltpu.VMEM((3 * k, 2 * k), f32),
        pltpu.VMEM((3 * k, k), f32),
        pltpu.VMEM((3 * k, k), f32),
        pltpu.VMEM((3 * k, 3 * k), f32),
        pltpu.VMEM((3 * k, 3 * k), f32),
        dma((4,)),
        dma((2, 4)), dma((2, 4)),
        dma((2, 2)), dma((2, 2)),
        dma((3, GROUP - 1, levels)), dma((3, GROUP - 1, levels)),
        dma((3, levels - 1)), dma((3, levels - 1)),
        dma((3, levels - 1)), dma((3, levels - 1)),
        dma((3, levels, GROUP - 1)), dma((3, levels, GROUP - 1)),
        dma((5,)), dma((5,)),
        dma((3,)),
    ]
    image_t, grams = pl.pallas_call(
        functools.partial(step_kernel, count, factor),
        out_shape=(jax.ShapeDtypeStruct((3 * k, depth), bf16), jax.ShapeDtypeStruct((2, 3 * k, 3 * k), f32)),
        in_specs=[pl.BlockSpec(memory_space=pl.ANY), vmem, vmem],
        out_specs=(pl.BlockSpec(memory_space=pl.ANY), vmem),
        scratch_shapes=scratch,
        compiler_params=pltpu.CompilerParams(
            collective_id=0, has_side_effects=True, vmem_limit_bytes=56 * 1024 * 1024
        ),
        cost_estimate=pl.CostEstimate(
            flops=12 * rows * depth * k, bytes_accessed=2 * rows * depth, transcendentals=0
        ),
        name="lobpcg_step",
    )(hidden_states, current_block.T, directions.T)
    return image_t.astype(f32).T, grams[0], grams[1]


def solution(mesh):
    def program(hidden_states, current_block, directions):
        count, halves = mesh.shape["tok"], mesh.shape["feat"]
        depth = hidden_states.shape[1] // halves
        whole_tiles = count % GROUP == 0 and count > GROUP and depth % (128 * count) == 0
        return jax.shard_map(
            local_kernel if halves == 2 and whole_tiles else local,
            mesh=mesh,
            in_specs=(P("tok", "feat"), P("feat", None), P("feat", None)),
            out_specs=(P("feat", None), P(), P()),
            check_vma=False,
        )(hidden_states, current_block, directions)

    return program
```
